256 devices in a mesh: sub: 32 (over x, z_lo, core), sec: 8 (over y, z_hi).
Axes of the slice: x: 4, y: 4, z: 8 (z_hi: 2, z_lo: 4; z = z_hi * 4 + z_lo), core: 2. Of those that a mesh axis runs over, the one named last changes fastest.
Arguments:
- image: bfloat16 [32, 2, 2048, 512], P('sub', None, 'sec'), may hold values from -6 to 6
- range_offsets: int32 [32, 3, 2, 4], P('sub'), may hold values from 0 to 16
- tap_weights: bfloat16 [32, 3, 2, 128, 8], P('sub'), may hold values from -1.1953125 to 1.1953125
- beam_weights: float32 [32, 3, 2, 4], P('sub'), may hold values from 0.25 to 1
- phase_rates: float32 [32, 3, 2], P('sub'), may hold values from 1 to 40
Outputs:
- merged: bfloat16 [32, 2, 2048, 512], P('sub', None, 'sec')
The draws below stay inside these ranges and needn't reach their ends.
All inputs are finite; a program needn't handle non-finite values.
Results may differ from the reference program's by a relative error of at most 0.0043.
Values may be sent and summed in bfloat16 or wider, within the bound.
No kernel may reach another device: no remote copies, remote signals or barrier semaphores. Data moves between devices by JAX's collectives and lax.ppermute only.
A program may use at most 64 MiB of HBM per device.

```python
import math
import jax
import jax.numpy as jnp
from jax import lax

RANGE = 512
SECTIONS = 3
BLOCK = 128
TAPS = 8
MARGIN_ROWS = 12
SUBAPERTURES = 32
BEAMS = 2048
BLOCKS = 4
N_SUB = 32


def with_ends(drawn, own_key, least, top_value):
    index_at = [jax.random.randint(jax.random.fold_in(own_key, axis), (), 0, length) for axis, length in enumerate(drawn.shape)]
    widest = drawn.shape.index(max(drawn.shape))
    next_to = index_at[:widest] + [(index_at[widest] + 1) % drawn.shape[widest]] + index_at[widest + 1:]
    return drawn.at[tuple(index_at)].set(least).at[tuple(next_to)].set(top_value)


def levels(key, shape, shards, least, largest):
    gain, own = 1.0, jax.random.fold_in(key, 6)
    for position, parts in shards:
        draws = jnp.exp(jax.random.uniform(jax.random.fold_in(own, position), (parts,), jnp.float32, least / len(shards), largest / len(shards)))
        gain = gain * jnp.repeat(draws, shape[position] // parts).reshape([-1 if axis == position else 1 for axis in range(len(shape))])
    return gain


def gaussian(stream_key, extent, deviation, limit, pieces=(), kind=jnp.bfloat16):
    factor_of = levels(stream_key, extent, pieces, -0.22, 0.18) if pieces else 1.0
    values = jax.random.normal(stream_key, extent, jnp.float32) * deviation * factor_of
    return jnp.minimum(jnp.maximum(values, -limit), limit).astype(kind)


def setup_inputs(seed: int = 0) -> dict:
    arg_keys = jax.random.split(jax.random.key(seed), 6)
    image = gaussian(arg_keys[0], (SUBAPERTURES, 2, BEAMS, RANGE), 1.0, 6.0, ((0, 32), (2, 8)))
    range_offsets = with_ends(jax.random.randint(arg_keys[1], (SUBAPERTURES, SECTIONS, 2, BLOCKS), 0, 2 * MARGIN_ROWS - TAPS + 1), jax.random.fold_in(arg_keys[1], 1), 0, 2 * MARGIN_ROWS - TAPS).astype(jnp.int32)
    tap_weights = gaussian(arg_keys[2], (SUBAPERTURES, SECTIONS, 2, BLOCK, TAPS), 0.2, 1.1953125, ((0, 32),))
    beam_weights = jnp.clip(0.25 + 0.75 * jax.random.uniform(arg_keys[3], (SUBAPERTURES, SECTIONS, 2, 4), jnp.float32) ** levels(arg_keys[3], (SUBAPERTURES, SECTIONS, 2, 4), ((0, 32),), -0.2, 0.2), 0.25, 1.0)
    phase_rates = jnp.clip(jnp.exp(math.log(40.0) - 3.6888795 * jax.random.uniform(arg_keys[4], (SUBAPERTURES, SECTIONS, 2), jnp.float32) ** levels(arg_keys[4], (SUBAPERTURES, SECTIONS, 2), ((0, 32),), -0.2, 0.2)), 1.0, 40.0)
    return dict(image=image, range_offsets=range_offsets, tap_weights=tap_weights, beam_weights=beam_weights, phase_rates=phase_rates)


def contribute(child, offsets, tap_weights, beam_weights, phase_rate):
    beams = child.shape[1]
    padded = jnp.pad(child, ((0, 0), (2, 2), (MARGIN_ROWS, MARGIN_ROWS)))
    starts = jnp.arange(RANGE // BLOCK, dtype=jnp.int32) * BLOCK + offsets.astype(jnp.int32)
    windows = jax.vmap(lambda start: lax.dynamic_slice_in_dim(padded, start, BLOCK + TAPS, 2))(starts)
    taps_wide = tap_weights.astype(jnp.float32)
    interp = jnp.zeros(windows.shape[:3] + (BLOCK,), jnp.float32)
    for tap_idx in range(TAPS):
        interp = interp + windows[..., tap_idx:tap_idx + BLOCK].astype(jnp.float32) * taps_wide[:, tap_idx]
    interp = jnp.transpose(interp, (1, 2, 0, 3)).reshape(2, beams + 4, RANGE)
    blended = jnp.zeros((2, beams, RANGE), jnp.float32)
    for angle_idx in range(4):
        blended = blended + beam_weights[angle_idx] * interp[:, 1 + angle_idx:1 + angle_idx + beams]
    beam_idx = jnp.arange(beams, dtype=jnp.int32).astype(jnp.float32)
    range_idx = jnp.arange(RANGE, dtype=jnp.int32).astype(jnp.float32)
    phase = phase_rate * ((beam_idx[:, None] + 1.0) * (range_idx[None, :] + 1.0)) / (RANGE * beams)
    cosine = jnp.cos(phase)
    sine = jnp.sin(phase)
    return jnp.stack([cosine * blended[0] - sine * blended[1], sine * blended[0] + cosine * blended[1]])


def reference(image, range_offsets, tap_weights, beam_weights, phase_rates):
    subimages = image
    positions = jnp.arange(N_SUB, dtype=jnp.int32)
    for section_idx in range(SECTIONS):
        partners = jnp.bitwise_xor(positions, 2 ** section_idx)

        def merge_one(sub_idx, current=subimages, section_idx=section_idx, partners=partners):
            own_part = contribute(current[sub_idx], range_offsets[sub_idx, section_idx, 0],
                                  tap_weights[sub_idx, section_idx, 0], beam_weights[sub_idx, section_idx, 0],
                                  phase_rates[sub_idx, section_idx, 0])
            far_part = contribute(current[partners[sub_idx]], range_offsets[sub_idx, section_idx, 1],
                                  tap_weights[sub_idx, section_idx, 1], beam_weights[sub_idx, section_idx, 1],
                                  phase_rates[sub_idx, section_idx, 1])
            return (own_part + far_part).astype(jnp.bfloat16)

        subimages = lax.map(merge_one, positions)
    return subimages
```

```python
import functools
import math
import jax
import jax.numpy as jnp
from jax import lax
from jax.experimental import pallas as pl
from jax.experimental.pallas import tpu as pltpu
from jax.sharding import PartitionSpec as P

SECTIONS = 3
BLOCK = 128
TAPS = 8
MARGIN_ROWS = 12
VMEM_LIMIT = 40 * 1024 * 1024
SMALL_COST = pl.CostEstimate(flops=1000, bytes_accessed=1000, transcendentals=0)


def sin_cos(angle):
    quadrant = jnp.floor(angle * (2.0 / math.pi) + 0.5)
    rest = angle - quadrant * 1.5703125
    rest = rest - quadrant * 4.8375129699707031e-4
    rest = rest - quadrant * 7.5495690e-8
    square = rest * rest
    sine = rest + rest * square * (
        -1.6666654611e-1 + square * (8.3321608736e-3 - square * 1.9515295891e-4)
    )
    cosine = 1.0 - 0.5 * square + square * square * (
        4.166664568298827e-2 + square * (-1.388731625493765e-3 + square * 2.443315711809948e-5)
    )
    turn = quadrant.astype(jnp.int32)
    odd = (turn & 1) == 1
    sin_value = jnp.where(odd, cosine, sine)
    cos_value = jnp.where(odd, sine, cosine)
    sin_value = jnp.where((turn & 2) == 2, -sin_value, sin_value)
    cos_value = jnp.where(((turn + 1) & 2) == 2, -cos_value, cos_value)
    return sin_value, cos_value


def band_kernel(offsets_ref, taps_ref, *out_refs):
    blocks = offsets_ref.shape[3]
    length = blocks * BLOCK
    row = lax.broadcasted_iota(jnp.int32, (16, BLOCK), 0)
    lane = lax.broadcasted_iota(jnp.int32, (16, BLOCK), 1)
    diff = row - lane
    for s, out_ref in enumerate(out_refs):
        out_ref[...] = jnp.zeros(out_ref.shape, out_ref.dtype)
        for j in range(2):
            taps = taps_ref[0, s, j].astype(jnp.float32)
            for n in range(blocks):
                base = offsets_ref[0, s, j, n] - MARGIN_ROWS
                for first in range(-16, BLOCK + 16, 16):
                    place = n * BLOCK + first
                    if place < 0 or place >= length:
                        continue
                    shift = diff + (first - base)
                    value = jnp.zeros((16, BLOCK), jnp.float32)
                    for t in range(TAPS):
                        value = jnp.where(shift == t, taps[t : t + 1, :], value)
                    out_ref[j, place : place + 16, n * BLOCK : (n + 1) * BLOCK] = value.astype(
                        out_ref.dtype
                    )


def make_bands(range_offsets, taps, length):
    vmem = pl.BlockSpec(memory_space=pltpu.VMEM)
    return pl.pallas_call(
        band_kernel,
        out_shape=[jax.ShapeDtypeStruct((2, length, length), jnp.bfloat16)] * SECTIONS,
        in_specs=[pl.BlockSpec(memory_space=pltpu.SMEM), vmem],
        out_specs=[vmem] * SECTIONS,
        compiler_params=pltpu.CompilerParams(vmem_limit_bytes=VMEM_LIMIT),
        cost_estimate=SMALL_COST,
        name="bands",
    )(range_offsets, taps)


EDGE = 8


def pack_kernel(near_ref, far_ref, out_ref):
    even = lax.rem(lax.axis_index("sub"), 2) == 0
    for j, ref in enumerate((near_ref, far_ref)):
        for z in range(2):
            rows = ref[0, z].astype(jnp.float32)
            rows = jnp.where(even, rows[EDGE:], rows[:EDGE])
            out_ref[j, z] = rows.astype(out_ref.dtype)


def pack_edges(near, far):
    vmem = pl.BlockSpec(memory_space=pltpu.VMEM)
    return pl.pallas_call(
        pack_kernel,
        out_shape=jax.ShapeDtypeStruct((2, 2, EDGE, near.shape[3]), near.dtype),
        in_specs=[vmem] * 2,
        out_specs=vmem,
        compiler_params=pltpu.CompilerParams(vmem_limit_bytes=VMEM_LIMIT),
        cost_estimate=SMALL_COST,
        name="pack",
    )(near, far)


def relay_kernel(count, *refs):
    for source, target in zip(refs[:count], refs[-count:]):
        target[...] = source[...]


def relay(arrays, after):
    vmem = pl.BlockSpec(memory_space=pltpu.VMEM)
    return pl.pallas_call(
        functools.partial(relay_kernel, len(arrays)),
        out_shape=[jax.ShapeDtypeStruct(x.shape, x.dtype) for x in arrays],
        in_specs=[vmem] * len(arrays) + [pl.BlockSpec(memory_space=pl.ANY)] * len(after),
        out_specs=[vmem] * len(arrays),
        compiler_params=pltpu.CompilerParams(vmem_limit_bytes=VMEM_LIMIT),
        cost_estimate=SMALL_COST,
        name="relay",
    )(*arrays, *after)


def rows_of(ref, z, first, rows):
    return ref[(0,) * (len(ref.shape) - 3) + (z, slice(first, first + rows))]


def merge_kernel(s, slices, windows, masked, sector, total, pieces, edges, partial, kept, unread, *refs):
    weights_ref, rates_ref, bands_ref = refs[:3]
    own_refs = refs[3 : 3 + pieces]
    far_refs = refs[3 + pieces : 3 + 2 * pieces]
    rest = refs[3 + 2 * pieces :]
    if edges:
        near_edges_ref, swapped_edges_ref, *rest = rest
    kept_refs, rest = rest[: len(kept)], rest[len(kept) + unread :]
    out_ref, rows_ref, interp_ref, *rest = rest
    if partial:
        hbm_ref, (out_ref, sems) = out_ref, rest
        copies = []

        def send(source, part):
            copies.append(pltpu.make_async_copy(source, hbm_ref.at[part], sems.at[len(copies)]))
            copies[-1].start()

        for ref, (first, rows) in zip(kept_refs, kept):
            send(ref, (slice(None), pl.ds(first, rows)))
    length = bands_ref.shape[1]
    blocks = length // BLOCK
    count = sum(item[2] for item in slices)
    place_in_sec = lax.axis_index("sec")
    first_beam = place_in_sec * sector
    even = lax.rem(lax.axis_index("sub"), 2) == 0

    for j, piece_refs in enumerate((own_refs, far_refs)):
        for z in range(2):
            place = z * count
            for piece, first, rows, _ in slices:
                if piece in ("low", "high"):
                    low = piece == "low"
                    near = even if low else jnp.logical_not(even)
                    end = 0 if low else lax.axis_size("sec") - 1
                    inner = place_in_sec != end
                    target = slice(place, place + rows)

                    def put(ref, child, z=z, low=low, target=target):
                        beams = ref[child, z].astype(jnp.float32)
                        blank = jnp.zeros_like(beams)
                        both = [blank, beams] if low else [beams, blank]
                        rows_ref[target, :] = jnp.concatenate(both, axis=0).astype(rows_ref.dtype)

                    @pl.when(jnp.logical_and(inner, near))
                    def _(put=put, j=j):
                        put(near_edges_ref, j)

                    @pl.when(jnp.logical_and(inner, jnp.logical_not(near)))
                    def _(put=put, j=j):
                        put(swapped_edges_ref, 1 - j)

                    @pl.when(jnp.logical_not(inner))
                    def _(target=target, rows=rows):
                        rows_ref[target, :] = jnp.zeros((rows, length), rows_ref.dtype)

                else:
                    rows_ref[place : place + rows, :] = rows_of(piece_refs[piece], z, first, rows)
                place += rows
        product = jnp.dot(rows_ref[...], bands_ref[j], preferred_element_type=jnp.float32)
        for z in range(2):
            place = z * count
            for _, _, rows, target in slices:
                for n in range(blocks):
                    interp_ref[j, z, n, target : target + rows, :] = product[
                        place : place + rows, n * BLOCK : (n + 1) * BLOCK
                    ]
                place += rows
            for _, rows, _, scratch_row in windows:
                top = max(t + r for _, _, r, t in slices if t <= scratch_row + rows)
                if top < scratch_row + rows + 2:
                    interp_ref[j, z, :, top : top + 8, :] = jnp.zeros((blocks, 8, BLOCK), jnp.float32)

    scale = 1.0 / (length * total)
    lane = lax.broadcasted_iota(jnp.int32, (16, BLOCK), 1)
    row = lax.broadcasted_iota(jnp.int32, (16, BLOCK), 0)
    steps = []
    for j in range(2):
        rate = rates_ref[0, j, s]
        for n in range(blocks):
            range_idx = (lane[:8] + (n * BLOCK + 1)).astype(jnp.float32)
            steps.append(sin_cos(rate * (16.0 * range_idx) * scale))
    factors = [[weights_ref[0, s, j, a] for a in range(4)] for j in range(2)]

    for out_row, rows, beam, scratch_row in windows:
        start_tables = []
        beam_idx = (row + (first_beam + beam + 1)).astype(jnp.float32)
        for j in range(2):
            rate = rates_ref[0, j, s]
            for n in range(blocks):
                range_idx = (lane + (n * BLOCK + 1)).astype(jnp.float32)
                start_tables.append(sin_cos(rate * (beam_idx * range_idx) * scale))

        def step(i, tables, out_row=out_row, beam=beam, scratch_row=scratch_row):
            later = []
            if masked:
                at = row + (first_beam + beam + 16 * i)
                inside = (at >= 0) & (at < total)
            sums = [[None, None] for _ in range(blocks)]
            for j in range(2):
                for n in range(blocks):
                    sine, cosine = tables[j * blocks + n]
                    parts = []
                    for z in range(2):
                        acc = None
                        for a in range(4):
                            term = factors[j][a] * interp_ref[
                                j, z, n, pl.ds(scratch_row - 1 + a + 16 * i, 16), :
                            ]
                            acc = term if acc is None else acc + term
                        parts.append(acc)
                    real = cosine * parts[0] - sine * parts[1]
                    imag = sine * parts[0] + cosine * parts[1]
                    if j == 0:
                        sums[n] = [real, imag]
                    else:
                        sums[n] = [sums[n][0] + real, sums[n][1] + imag]
                    step_sine, step_cosine = steps[j * blocks + n]
                    step_sine = jnp.concatenate([step_sine, step_sine], axis=0)
                    step_cosine = jnp.concatenate([step_cosine, step_cosine], axis=0)
                    later.append(
                        (
                            sine * step_cosine + cosine * step_sine,
                            cosine * step_cosine - sine * step_sine,
                        )
                    )
            for n in range(blocks):
                for z in range(2):
                    value = sums[n][z]
                    if masked:
                        value = jnp.where(inside, value, 0.0)
                    target = out_row + 16 * i
                    if not isinstance(target, int):
                        target = pl.multiple_of(target, 16)
                    out_ref[z, pl.ds(target, 16), n * BLOCK : (n + 1) * BLOCK] = value.astype(
                        out_ref.dtype
                    )
            return later

        lax.fori_loop(0, rows // 16, step, start_tables)
        if partial:
            part = (slice(None), pl.ds(out_row, rows))
            send(out_ref.at[part], part)
    if partial:
        for copy in copies:
            copy.wait()


def merge(s, own, far, windows, out_rows, args, masked=False, edges=None, partial=0, after=(), kept=()):
    sector, total, weights, rates, bands = args
    length = own[0].shape[-1]
    placed_slices = []
    placed_windows = []
    base = 0
    for out_row, rows, beam, pieces in windows:
        lead = max(pieces, key=lambda item: item[2])[3] - beam
        low = min(item[3] for item in pieces) - beam
        origin = base + max(8, -low)
        origin += -(origin + lead) % 8
        top = origin + rows + 10
        for piece, first, count, at in pieces:
            placed_slices.append((piece, first, count, origin + at - beam))
            top = max(top, origin + at - beam + count)
        placed_windows.append((out_row, rows, beam, origin))
        base = -(-top // 8) * 8
    count = sum(item[2] for item in placed_slices)
    operands = [weights, rates, bands[s], *own, *far, *(edges or ())]
    operands.extend(item[0] for item in kept)
    operands.extend(after)
    kernel = functools.partial(
        merge_kernel,
        s,
        placed_slices,
        placed_windows,
        masked,
        sector,
        total,
        len(own),
        edges is not None,
        partial,
        [item[1:] for item in kept],
        len(after),
    )
    vmem = pl.BlockSpec(memory_space=pltpu.VMEM)
    smem = pl.BlockSpec(memory_space=pltpu.SMEM)
    out_shape = jax.ShapeDtypeStruct((2, out_rows, length), jnp.bfloat16)
    in_specs = [smem, smem] + [vmem] * (len(operands) - 2)
    scratch = [
        pltpu.VMEM((2 * count, length), jnp.bfloat16),
        pltpu.VMEM((2, 2, length // BLOCK, base + 8, BLOCK), jnp.float32),
    ]
    if partial:
        scratch += [
            pltpu.VMEM((2, out_rows, length), jnp.bfloat16),
            pltpu.SemaphoreType.DMA((len(kept) + len(windows),)),
        ]
    anywhere = pl.BlockSpec(memory_space=pl.ANY)
    if after:
        in_specs[-len(after) :] = [anywhere] * len(after)
    return pl.pallas_call(
        kernel,
        out_shape=out_shape,
        in_specs=in_specs,
        out_specs=anywhere if partial else vmem,
        scratch_shapes=scratch,
        compiler_params=pltpu.CompilerParams(vmem_limit_bytes=VMEM_LIMIT),
        cost_estimate=SMALL_COST,
        name=f"merge{s}",
    )(*operands)


def to_sectors(x):
    subs, secs = lax.axis_size("sub"), lax.axis_size("sec")
    pairs = []
    for sub in range(subs):
        step = 1 if sub % 2 == 0 else -1
        for sec in range(secs):
            pairs.append((sub * secs + sec, sub * secs + (sec + step) % secs))
    return lax.ppermute(x, ("sub", "sec"), pairs)


def from_partner(x, bit):
    return lax.ppermute(x, "sub", [(i, i ^ 1 << bit) for i in range(lax.axis_size("sub"))])


def body(image, range_offsets, tap_weights, beam_weights, phase_rates):
    sector, length = image.shape[2:]
    total = sector * lax.axis_size("sec")
    far = from_partner(image, 0)
    taps = jnp.swapaxes(tap_weights, 3, 4)
    rates = jnp.swapaxes(phase_rates, 1, 2)
    bands = make_bands(range_offsets, taps, length)
    edges = jnp.concatenate([image[:, :, :EDGE], image[:, :, sector - EDGE :]], axis=2)
    near_edges = to_sectors(pack_edges(edges, from_partner(edges, 0)))
    (near_edges,) = relay((near_edges,), (bands[1], beam_weights, rates))
    swapped_edges = from_partner(near_edges, 0)
    args = (sector, total, beam_weights, rates, bands)

    mid1a = merge(
        0, [image], [far], [(0, 96, 30, [(0, 16, 112, 16)])], 96, args, after=(swapped_edges,)
    )
    mid1b = merge(0, [image], [far], [(0, 96, 126, [(0, 112, 112, 112)])], 96, args, after=(mid1a,))
    ends1 = merge(
        0,
        [image],
        [far],
        [
            (0, 32, -2, [("low", 0, 16, -16), (0, 0, 32, 0)]),
            (32, 48, 212, [(0, 208, 48, 208), ("high", 0, 16, 256)]),
        ],
        80,
        args,
        masked=True,
        edges=(near_edges, swapped_edges),
        after=(mid1b,),
    )
    far_ends1 = from_partner(ends1, 1)
    far_mid1b = from_partner(mid1b, 1)
    far_mid1a = from_partner(mid1a, 1)
    mid2a = merge(
        1, [mid1a], [far_mid1a], [(0, 96, 31, [(0, 0, 96, 30)])], 96, args, after=(ends1,)
    )
    mid2b = merge(
        1,
        [mid1b, mid1a],
        [far_mid1b, far_mid1a],
        [(0, 96, 124, [(1, 80, 16, 110), (0, 0, 96, 126)])],
        96,
        args,
        after=(mid2a,),
    )
    ends2 = merge(
        1,
        [ends1, mid1b, mid1a],
        [far_ends1, far_mid1b, far_mid1a],
        [
            (0, 32, -1, [(0, 0, 32, -2), (2, 0, 16, 30)]),
            (32, 48, 210, [(1, 80, 16, 206), (0, 32, 48, 212)]),
        ],
        80,
        args,
        masked=True,
        after=(mid2b,),
    )
    far_ends2 = from_partner(ends2, 2)
    far_mid2b = from_partner(mid2b, 2)
    far_mid2a = from_partner(mid2a, 2)
    part3a = merge(
        2, [mid2a], [far_mid2a], [(0, 80, 32, [(0, 0, 96, 31)])], 80, args, after=(ends2,)
    )
    part3b = merge(
        2,
        [mid2b, mid2a],
        [far_mid2b, far_mid2a],
        [(0, 96, 112, [(1, 80, 16, 111), (0, 0, 96, 124)])],
        96,
        args,
        after=(part3a,),
    )
    merged = merge(
        2,
        [ends2, mid2b, mid2a],
        [far_ends2, far_mid2b, far_mid2a],
        [
            (0, 32, 0, [(0, 0, 32, -1), (2, 0, 16, 31)]),
            (208, 48, 208, [(1, 80, 16, 204), (0, 32, 48, 210)]),
        ],
        sector,
        args,
        partial=1,
        kept=[(part3a, 32, 80), (part3b, 112, 96)],
    )
    return merged[None]


def solution(mesh):
    in_specs = (
        P("sub", None, "sec", None),
        P("sub", None, None, None),
        P("sub", None, None, None, None),
        P("sub", None, None, None),
        P("sub", None, None),
    )
    out_specs = P("sub", None, "sec", None)
    return jax.shard_map(body, mesh=mesh, in_specs=in_specs, out_specs=out_specs, check_vma=False)
```

```python
import functools
import math
import jax
import jax.numpy as jnp
from jax import lax
from jax.experimental import pallas as pl
from jax.experimental.pallas import tpu as pltpu
from jax.sharding import PartitionSpec as P

SECTIONS = 3
BLOCK = 128
TAPS = 8
MARGIN_ROWS = 12
VMEM_LIMIT = 40 * 1024 * 1024
MERGE_COST = pl.CostEstimate(flops=800_000_000, bytes_accessed=1000, transcendentals=0)
SMALL_COST = pl.CostEstimate(flops=1000, bytes_accessed=1000, transcendentals=0)


def sin_cos(angle):
    quadrant = jnp.floor(angle * (2.0 / math.pi) + 0.5)
    rest = angle - quadrant * 1.5703125
    rest = rest - quadrant * 4.8375129699707031e-4
    rest = rest - quadrant * 7.5495690e-8
    square = rest * rest
    sine = rest + rest * square * (
        -1.6666654611e-1 + square * (8.3321608736e-3 - square * 1.9515295891e-4)
    )
    cosine = 1.0 - 0.5 * square + square * square * (
        4.166664568298827e-2 + square * (-1.388731625493765e-3 + square * 2.443315711809948e-5)
    )
    turn = quadrant.astype(jnp.int32)
    odd = (turn & 1) == 1
    sin_value = jnp.where(odd, cosine, sine)
    cos_value = jnp.where(odd, sine, cosine)
    sin_value = jnp.where((turn & 2) == 2, -sin_value, sin_value)
    cos_value = jnp.where(((turn + 1) & 2) == 2, -cos_value, cos_value)
    return sin_value, cos_value


def band_kernel(offsets_ref, taps_ref, image_ref, *out_refs):
    out_refs[-1][...] = image_ref[...]
    blocks = offsets_ref.shape[3]
    length = blocks * BLOCK
    row = lax.broadcasted_iota(jnp.int32, (16, BLOCK), 0)
    lane = lax.broadcasted_iota(jnp.int32, (16, BLOCK), 1)
    diff = row - lane
    for s, out_ref in enumerate(out_refs[:-1]):
        out_ref[...] = jnp.zeros(out_ref.shape, out_ref.dtype)
        for j in range(2):
            taps = taps_ref[0, s, j].astype(jnp.float32)
            for n in range(blocks):
                base = offsets_ref[0, s, j, n] - MARGIN_ROWS
                for first in range(-16, BLOCK + 16, 16):
                    place = n * BLOCK + first
                    if place < 0 or place >= length:
                        continue
                    shift = diff + (first - base)
                    value = jnp.zeros((16, BLOCK), jnp.float32)
                    for t in range(TAPS):
                        value = jnp.where(shift == t, taps[t : t + 1, :], value)
                    out_ref[j, place : place + 16, n * BLOCK : (n + 1) * BLOCK] = value.astype(
                        out_ref.dtype
                    )


def make_bands(range_offsets, taps, image):
    length = image.shape[3]
    vmem = pl.BlockSpec(memory_space=pltpu.VMEM)
    return pl.pallas_call(
        band_kernel,
        out_shape=[jax.ShapeDtypeStruct((2, length, length), jnp.bfloat16)] * SECTIONS
        + [jax.ShapeDtypeStruct(image.shape, image.dtype)],
        in_specs=[pl.BlockSpec(memory_space=pltpu.SMEM), vmem, vmem],
        out_specs=[vmem] * (SECTIONS + 1),
        compiler_params=pltpu.CompilerParams(vmem_limit_bytes=VMEM_LIMIT),
        cost_estimate=SMALL_COST,
        name="bands",
    )(range_offsets, taps, image)


EDGE = 8


def pack_kernel(near_ref, far_ref, out_ref):
    even = lax.rem(lax.axis_index("sub"), 2) == 0
    for j, ref in enumerate((near_ref, far_ref)):
        for z in range(2):
            rows = ref[0, z].astype(jnp.float32)
            rows = jnp.where(even, rows[EDGE:], rows[:EDGE])
            out_ref[j, z] = rows.astype(out_ref.dtype)


def pack_edges(near, far):
    vmem = pl.BlockSpec(memory_space=pltpu.VMEM)
    return pl.pallas_call(
        pack_kernel,
        out_shape=jax.ShapeDtypeStruct((2, 2, EDGE, near.shape[3]), near.dtype),
        in_specs=[vmem] * 2,
        out_specs=vmem,
        compiler_params=pltpu.CompilerParams(vmem_limit_bytes=VMEM_LIMIT),
        cost_estimate=SMALL_COST,
        name="pack",
    )(near, far)


def relay_kernel(count, *refs):
    for source, target in zip(refs[:count], refs[-count:]):
        target[...] = source[...]


def relay(arrays, after):
    vmem = pl.BlockSpec(memory_space=pltpu.VMEM)
    return pl.pallas_call(
        functools.partial(relay_kernel, len(arrays)),
        out_shape=[jax.ShapeDtypeStruct(x.shape, x.dtype) for x in arrays],
        in_specs=[vmem] * len(arrays) + [pl.BlockSpec(memory_space=pl.ANY)] * len(after),
        out_specs=[vmem] * len(arrays),
        compiler_params=pltpu.CompilerParams(vmem_limit_bytes=VMEM_LIMIT),
        cost_estimate=SMALL_COST,
        name="relay",
    )(*arrays, *after)


def rows_of(ref, z, first, rows):
    return ref[(0,) * (len(ref.shape) - 3) + (z, slice(first, first + rows))]


def merge_kernel(s, slices, windows, masked, sector, total, pieces, edges, partial, kept, unread, *refs):
    weights_ref, rates_ref, bands_ref = refs[:3]
    own_refs = refs[3 : 3 + pieces]
    far_refs = refs[3 + pieces : 3 + 2 * pieces]
    rest = refs[3 + 2 * pieces :]
    if edges:
        near_edges_ref, swapped_edges_ref, *rest = rest
    kept_refs, rest = rest[: len(kept)], rest[len(kept) + unread :]
    out_ref, rows_ref, interp_ref, *rest = rest
    if partial:
        hbm_ref, (out_ref, sems) = out_ref, rest
        copies = []

        def send(source, part):
            copies.append(pltpu.make_async_copy(source, hbm_ref.at[part], sems.at[len(copies)]))
            copies[-1].start()

        for ref, (first, rows) in zip(kept_refs, kept):
            send(ref, (slice(None), pl.ds(first, rows)))
    length = bands_ref.shape[1]
    blocks = length // BLOCK
    count = sum(item[2] for item in slices)
    place_in_sec = lax.axis_index("sec")
    first_beam = place_in_sec * sector
    even = lax.rem(lax.axis_index("sub"), 2) == 0

    for j, piece_refs in enumerate((own_refs, far_refs)):
        for z in range(2):
            place = z * count
            for piece, first, rows, _ in slices:
                if piece in ("low", "high"):
                    low = piece == "low"
                    near = even if low else jnp.logical_not(even)
                    end = 0 if low else lax.axis_size("sec") - 1
                    inner = place_in_sec != end
                    target = slice(place, place + rows)

                    def put(ref, child, z=z, low=low, target=target):
                        beams = ref[child, z].astype(jnp.float32)
                        blank = jnp.zeros_like(beams)
                        both = [blank, beams] if low else [beams, blank]
                        rows_ref[target, :] = jnp.concatenate(both, axis=0).astype(rows_ref.dtype)

                    @pl.when(jnp.logical_and(inner, near))
                    def _(put=put, j=j):
                        put(near_edges_ref, j)

                    @pl.when(jnp.logical_and(inner, jnp.logical_not(near)))
                    def _(put=put, j=j):
                        put(swapped_edges_ref, 1 - j)

                    @pl.when(jnp.logical_not(inner))
                    def _(target=target, rows=rows):
                        rows_ref[target, :] = jnp.zeros((rows, length), rows_ref.dtype)

                else:
                    rows_ref[place : place + rows, :] = rows_of(piece_refs[piece], z, first, rows)
                place += rows
        product = jnp.dot(rows_ref[...], bands_ref[j], preferred_element_type=jnp.float32)
        for z in range(2):
            place = z * count
            for _, _, rows, target in slices:
                for n in range(blocks):
                    interp_ref[j, z, n, target : target + rows, :] = product[
                        place : place + rows, n * BLOCK : (n + 1) * BLOCK
                    ]
                place += rows
            for _, rows, _, scratch_row in windows:
                top = max(t + r for _, _, r, t in slices if t <= scratch_row + rows)
                if top < scratch_row + rows + 2:
                    interp_ref[j, z, :, top : top + 8, :] = jnp.zeros((blocks, 8, BLOCK), jnp.float32)

    scale = 1.0 / (length * total)
    lane = lax.broadcasted_iota(jnp.int32, (16, BLOCK), 1)
    row = lax.broadcasted_iota(jnp.int32, (16, BLOCK), 0)
    steps = []
    for j in range(2):
        rate = jnp.broadcast_to(rates_ref[0, j : j + 1, s : s + 1], (8, BLOCK))
        for n in range(blocks):
            range_idx = (lane[:8] + (n * BLOCK + 1)).astype(jnp.float32)
            steps.append(sin_cos(rate * (16.0 * range_idx) * scale))
    factors = [
        [jnp.broadcast_to(weights_ref[0, s, j : j + 1, a : a + 1], (16, BLOCK)) for a in range(4)]
        for j in range(2)
    ]

    for out_row, rows, beam, scratch_row in windows:
        start_tables = []
        beam_idx = (row + (first_beam + beam + 1)).astype(jnp.float32)
        for j in range(2):
            rate = jnp.broadcast_to(rates_ref[0, j : j + 1, s : s + 1], (16, BLOCK))
            for n in range(blocks):
                range_idx = (lane + (n * BLOCK + 1)).astype(jnp.float32)
                start_tables.append(sin_cos(rate * (beam_idx * range_idx) * scale))

        def step(i, tables, out_row=out_row, beam=beam, scratch_row=scratch_row):
            later = []
            if masked:
                at = row + (first_beam + beam + 16 * i)
                inside = (at >= 0) & (at < total)
            sums = [[None, None] for _ in range(blocks)]
            for j in range(2):
                for n in range(blocks):
                    sine, cosine = tables[j * blocks + n]
                    parts = []
                    for z in range(2):
                        acc = None
                        for a in range(4):
                            term = factors[j][a] * interp_ref[
                                j, z, n, pl.ds(scratch_row - 1 + a + 16 * i, 16), :
                            ]
                            acc = term if acc is None else acc + term
                        parts.append(acc)
                    real = cosine * parts[0] - sine * parts[1]
                    imag = sine * parts[0] + cosine * parts[1]
                    if j == 0:
                        sums[n] = [real, imag]
                    else:
                        sums[n] = [sums[n][0] + real, sums[n][1] + imag]
                    step_sine, step_cosine = steps[j * blocks + n]
                    step_sine = jnp.concatenate([step_sine, step_sine], axis=0)
                    step_cosine = jnp.concatenate([step_cosine, step_cosine], axis=0)
                    later.append(
                        (
                            sine * step_cosine + cosine * step_sine,
                            cosine * step_cosine - sine * step_sine,
                        )
                    )
            for n in range(blocks):
                for z in range(2):
                    value = sums[n][z]
                    if masked:
                        value = jnp.where(inside, value, 0.0)
                    target = out_row + 16 * i
                    if not isinstance(target, int):
                        target = pl.multiple_of(target, 16)
                    out_ref[z, pl.ds(target, 16), n * BLOCK : (n + 1) * BLOCK] = value.astype(
                        out_ref.dtype
                    )
            return later

        lax.fori_loop(0, rows // 16, step, start_tables, unroll=True)
        if partial:
            part = (slice(None), pl.ds(out_row, rows))
            send(out_ref.at[part], part)
    if partial:
        for copy in copies:
            copy.wait()


def merge(s, own, far, windows, out_rows, args, masked=False, edges=None, partial=0, after=(), kept=()):
    sector, total, weights, rates, bands = args
    length = own[0].shape[-1]
    placed_slices = []
    placed_windows = []
    base = 0
    for out_row, rows, beam, pieces in windows:
        lead = max(pieces, key=lambda item: item[2])[3] - beam
        low = min(item[3] for item in pieces) - beam
        origin = base + max(8, -low)
        origin += -(origin + lead) % 8
        top = origin + rows + 10
        for piece, first, count, at in pieces:
            placed_slices.append((piece, first, count, origin + at - beam))
            top = max(top, origin + at - beam + count)
        placed_windows.append((out_row, rows, beam, origin))
        base = -(-top // 8) * 8
    count = sum(item[2] for item in placed_slices)
    operands = [weights, rates, bands[s], *own, *far, *(edges or ())]
    operands.extend(item[0] for item in kept)
    operands.extend(after)
    kernel = functools.partial(
        merge_kernel,
        s,
        placed_slices,
        placed_windows,
        masked,
        sector,
        total,
        len(own),
        edges is not None,
        partial,
        [item[1:] for item in kept],
        len(after),
    )
    vmem = pl.BlockSpec(memory_space=pltpu.VMEM)
    out_shape = jax.ShapeDtypeStruct((2, out_rows, length), jnp.bfloat16)
    in_specs = [vmem] * len(operands)
    scratch = [
        pltpu.VMEM((2 * count, length), jnp.bfloat16),
        pltpu.VMEM((2, 2, length // BLOCK, base + 8, BLOCK), jnp.float32),
    ]
    if partial:
        scratch += [
            pltpu.VMEM((2, out_rows, length), jnp.bfloat16),
            pltpu.SemaphoreType.DMA((len(kept) + len(windows),)),
        ]
    anywhere = pl.BlockSpec(memory_space=pl.ANY)
    if after:
        in_specs[-len(after) :] = [anywhere] * len(after)
    return pl.pallas_call(
        kernel,
        out_shape=out_shape,
        in_specs=in_specs,
        out_specs=anywhere if partial else vmem,
        scratch_shapes=scratch,
        compiler_params=pltpu.CompilerParams(vmem_limit_bytes=VMEM_LIMIT),
        cost_estimate=MERGE_COST,
        name=f"merge{s}",
    )(*operands)


def to_sectors(x):
    subs, secs = lax.axis_size("sub"), lax.axis_size("sec")
    pairs = []
    for sub in range(subs):
        step = 1 if sub % 2 == 0 else -1
        for sec in range(secs):
            pairs.append((sub * secs + sec, sub * secs + (sec + step) % secs))
    return lax.ppermute(x, ("sub", "sec"), pairs)


def from_partner(x, bit):
    return lax.ppermute(x, "sub", [(i, i ^ 1 << bit) for i in range(lax.axis_size("sub"))])


def body(image, range_offsets, tap_weights, beam_weights, phase_rates):
    sector = image.shape[2]
    total = sector * lax.axis_size("sec")
    far = from_partner(image, 0)
    taps = jnp.swapaxes(tap_weights, 3, 4)
    rates = jnp.swapaxes(phase_rates, 1, 2)
    *bands, near = make_bands(range_offsets, taps, image)
    edges = jnp.concatenate([image[:, :, :EDGE], image[:, :, sector - EDGE :]], axis=2)
    near_edges = to_sectors(pack_edges(edges, from_partner(edges, 0)))
    (near_edges,) = relay((near_edges,), (bands[1], beam_weights, rates))
    swapped_edges = from_partner(near_edges, 0)
    args = (sector, total, beam_weights, rates, bands)

    mid1a = merge(
        0, [near], [far], [(0, 64, 30, [(0, 16, 80, 16)])], 64, args, after=(near_edges,)
    )
    mid1b = merge(0, [near], [far], [(0, 64, 94, [(0, 80, 80, 80)])], 64, args, after=(mid1a,))
    mid1c = merge(0, [near], [far], [(0, 64, 158, [(0, 144, 80, 144)])], 64, args, after=(mid1b,))
    ends1 = merge(
        0,
        [near],
        [far],
        [
            (0, 32, -2, [("low", 0, 16, -16), (0, 0, 32, 0)]),
            (32, 48, 212, [(0, 208, 48, 208), ("high", 0, 16, 256)]),
        ],
        80,
        args,
        masked=True,
        edges=(near_edges, swapped_edges),
        after=(mid1c,),
    )
    far_ends1 = from_partner(ends1, 1)
    far_mid1c = from_partner(mid1c, 1)
    far_mid1b = from_partner(mid1b, 1)
    far_mid1a = from_partner(mid1a, 1)
    mid2a = merge(
        1, [mid1a], [far_mid1a], [(0, 64, 31, [(0, 0, 64, 30)])], 64, args, after=(ends1,)
    )
    mid2b = merge(
        1,
        [mid1b, mid1a],
        [far_mid1b, far_mid1a],
        [(0, 64, 92, [(1, 48, 16, 78), (0, 0, 64, 94)])],
        64,
        args,
        after=(mid2a,),
    )
    mid2c = merge(
        1,
        [mid1c, mid1b],
        [far_mid1c, far_mid1b],
        [(0, 64, 156, [(1, 48, 16, 142), (0, 0, 64, 158)])],
        64,
        args,
        after=(mid2b,),
    )
    ends2 = merge(
        1,
        [ends1, mid1c, mid1a],
        [far_ends1, far_mid1c, far_mid1a],
        [
            (0, 32, -1, [(0, 0, 32, -2), (2, 0, 16, 30)]),
            (32, 48, 210, [(1, 48, 16, 206), (0, 32, 48, 212)]),
        ],
        80,
        args,
        masked=True,
        after=(mid2c,),
    )
    far_ends2 = from_partner(ends2, 2)
    far_mid2c = from_partner(mid2c, 2)
    far_mid2b = from_partner(mid2b, 2)
    far_mid2a = from_partner(mid2a, 2)
    part3a = merge(
        2, [mid2a], [far_mid2a], [(0, 48, 32, [(0, 0, 64, 31)])], 48, args, after=(ends2,)
    )
    part3b = merge(
        2,
        [mid2b, mid2a],
        [far_mid2b, far_mid2a],
        [(0, 64, 80, [(1, 48, 16, 79), (0, 0, 64, 92)])],
        64,
        args,
        after=(part3a,),
    )
    part3c = merge(
        2,
        [mid2c, mid2b],
        [far_mid2c, far_mid2b],
        [(0, 64, 144, [(1, 48, 16, 140), (0, 0, 64, 156)])],
        64,
        args,
        after=(part3b,),
    )
    merged = merge(
        2,
        [ends2, mid2c, mid2a],
        [far_ends2, far_mid2c, far_mid2a],
        [
            (0, 32, 0, [(0, 0, 32, -1), (2, 0, 16, 31)]),
            (208, 48, 208, [(1, 48, 16, 204), (0, 32, 48, 210)]),
        ],
        sector,
        args,
        partial=1,
        kept=[(part3a, 32, 48), (part3b, 80, 64), (part3c, 144, 64)],
    )
    return merged[None]


def solution(mesh):
    in_specs = (
        P("sub", None, "sec", None),
        P("sub", None, None, None),
        P("sub", None, None, None, None),
        P("sub", None, None, None),
        P("sub", None, None),
    )
    out_specs = P("sub", None, "sec", None)
    return jax.shard_map(body, mesh=mesh, in_specs=in_specs, out_specs=out_specs, check_vma=False)
```

```python
import functools
import math
import jax
import jax.numpy as jnp
from jax import lax
from jax.experimental import pallas as pl
from jax.experimental.pallas import tpu as pltpu
from jax.sharding import PartitionSpec as P

SECTIONS = 3
BLOCK = 128
TAPS = 8
MARGIN_ROWS = 12
VMEM_LIMIT = 40 * 1024 * 1024
MERGE_COST = pl.CostEstimate(flops=800_000_000, bytes_accessed=1000, transcendentals=0)
SMALL_COST = pl.CostEstimate(flops=1000, bytes_accessed=1000, transcendentals=0)


def sin_cos(angle):
    quadrant = jnp.floor(angle * (2.0 / math.pi) + 0.5)
    rest = angle - quadrant * 1.5703125
    rest = rest - quadrant * 4.8375129699707031e-4
    rest = rest - quadrant * 7.5495690e-8
    square = rest * rest
    sine = rest + rest * square * (
        -1.6666654611e-1 + square * (8.3321608736e-3 - square * 1.9515295891e-4)
    )
    cosine = 1.0 - 0.5 * square + square * square * (
        4.166664568298827e-2 + square * (-1.388731625493765e-3 + square * 2.443315711809948e-5)
    )
    turn = quadrant.astype(jnp.int32)
    odd = (turn & 1) == 1
    sin_value = jnp.where(odd, cosine, sine)
    cos_value = jnp.where(odd, sine, cosine)
    sin_value = jnp.where((turn & 2) == 2, -sin_value, sin_value)
    cos_value = jnp.where(((turn + 1) & 2) == 2, -cos_value, cos_value)
    return sin_value, cos_value


def band_kernel(offsets_ref, taps_ref, image_ref, *out_refs):
    out_refs[-1][...] = image_ref[...]
    blocks = offsets_ref.shape[3]
    length = blocks * BLOCK
    row = lax.broadcasted_iota(jnp.int32, (16, BLOCK), 0)
    lane = lax.broadcasted_iota(jnp.int32, (16, BLOCK), 1)
    diff = row - lane
    for s, out_ref in enumerate(out_refs[:-1]):
        out_ref[...] = jnp.zeros(out_ref.shape, out_ref.dtype)
        for j in range(2):
            taps = taps_ref[0, s, j].astype(jnp.float32)
            for n in range(blocks):
                base = offsets_ref[0, s, j, n] - MARGIN_ROWS
                for first in range(-16, BLOCK + 16, 16):
                    place = n * BLOCK + first
                    if place < 0 or place >= length:
                        continue
                    shift = diff + (first - base)
                    value = jnp.zeros((16, BLOCK), jnp.float32)
                    for t in range(TAPS):
                        value = jnp.where(shift == t, taps[t : t + 1, :], value)
                    out_ref[j, place : place + 16, n * BLOCK : (n + 1) * BLOCK] = value.astype(
                        out_ref.dtype
                    )


def make_bands(range_offsets, taps, image):
    length = image.shape[3]
    vmem = pl.BlockSpec(memory_space=pltpu.VMEM)
    return pl.pallas_call(
        band_kernel,
        out_shape=[jax.ShapeDtypeStruct((2, length, length), jnp.bfloat16)] * SECTIONS
        + [jax.ShapeDtypeStruct(image.shape, image.dtype)],
        in_specs=[pl.BlockSpec(memory_space=pltpu.SMEM), vmem, vmem],
        out_specs=[vmem] * (SECTIONS + 1),
        compiler_params=pltpu.CompilerParams(vmem_limit_bytes=VMEM_LIMIT),
        cost_estimate=SMALL_COST,
        name="bands",
    )(range_offsets, taps, image)


EDGE = 8


def pack_kernel(near_ref, far_ref, out_ref):
    even = lax.rem(lax.axis_index("sub"), 2) == 0
    for j, ref in enumerate((near_ref, far_ref)):
        for z in range(2):
            rows = ref[0, z].astype(jnp.float32)
            rows = jnp.where(even, rows[EDGE:], rows[:EDGE])
            out_ref[j, z] = rows.astype(out_ref.dtype)


def pack_edges(near, far):
    vmem = pl.BlockSpec(memory_space=pltpu.VMEM)
    return pl.pallas_call(
        pack_kernel,
        out_shape=jax.ShapeDtypeStruct((2, 2, EDGE, near.shape[3]), near.dtype),
        in_specs=[vmem] * 2,
        out_specs=vmem,
        compiler_params=pltpu.CompilerParams(vmem_limit_bytes=VMEM_LIMIT),
        cost_estimate=SMALL_COST,
        name="pack",
    )(near, far)


def relay_kernel(count, *refs):
    for source, target in zip(refs[:count], refs[-count:]):
        target[...] = source[...]


def relay(arrays, after):
    vmem = pl.BlockSpec(memory_space=pltpu.VMEM)
    return pl.pallas_call(
        functools.partial(relay_kernel, len(arrays)),
        out_shape=[jax.ShapeDtypeStruct(x.shape, x.dtype) for x in arrays],
        in_specs=[vmem] * len(arrays) + [pl.BlockSpec(memory_space=pl.ANY)] * len(after),
        out_specs=[vmem] * len(arrays),
        compiler_params=pltpu.CompilerParams(vmem_limit_bytes=VMEM_LIMIT),
        cost_estimate=SMALL_COST,
        name="relay",
    )(*arrays, *after)


def rows_of(ref, z, first, rows):
    return ref[(0,) * (len(ref.shape) - 3) + (z, slice(first, first + rows))]


def merge_kernel(s, slices, windows, masked, sector, total, pieces, edges, partial, kept, unread, *refs):
    weights_ref, rates_ref, bands_ref = refs[:3]
    own_refs = refs[3 : 3 + pieces]
    far_refs = refs[3 + pieces : 3 + 2 * pieces]
    rest = refs[3 + 2 * pieces :]
    if edges:
        near_edges_ref, swapped_edges_ref, *rest = rest
    kept_refs, rest = rest[: len(kept)], rest[len(kept) + unread :]
    out_ref, rows_ref, interp_ref, *rest = rest
    if partial:
        hbm_ref, (out_ref, sems) = out_ref, rest
        copies = []

        def send(source, part):
            copies.append(pltpu.make_async_copy(source, hbm_ref.at[part], sems.at[len(copies)]))
            copies[-1].start()

        for ref, (first, rows) in zip(kept_refs, kept):
            send(ref, (slice(None), pl.ds(first, rows)))
    length = bands_ref.shape[1]
    blocks = length // BLOCK
    count = sum(item[2] for item in slices)
    place_in_sec = lax.axis_index("sec")
    first_beam = place_in_sec * sector
    even = lax.rem(lax.axis_index("sub"), 2) == 0

    for j, piece_refs in enumerate((own_refs, far_refs)):
        for z in range(2):
            place = z * count
            for piece, first, rows, _ in slices:
                if piece in ("low", "high"):
                    low = piece == "low"
                    near = even if low else jnp.logical_not(even)
                    end = 0 if low else lax.axis_size("sec") - 1
                    inner = place_in_sec != end
                    target = slice(place, place + rows)

                    def put(ref, child, z=z, low=low, target=target):
                        beams = ref[child, z].astype(jnp.float32)
                        blank = jnp.zeros_like(beams)
                        both = [blank, beams] if low else [beams, blank]
                        rows_ref[target, :] = jnp.concatenate(both, axis=0).astype(rows_ref.dtype)

                    @pl.when(jnp.logical_and(inner, near))
                    def _(put=put, j=j):
                        put(near_edges_ref, j)

                    @pl.when(jnp.logical_and(inner, jnp.logical_not(near)))
                    def _(put=put, j=j):
                        put(swapped_edges_ref, 1 - j)

                    @pl.when(jnp.logical_not(inner))
                    def _(target=target, rows=rows):
                        rows_ref[target, :] = jnp.zeros((rows, length), rows_ref.dtype)

                else:
                    rows_ref[place : place + rows, :] = rows_of(piece_refs[piece], z, first, rows)
                place += rows
        product = jnp.dot(rows_ref[...], bands_ref[j], preferred_element_type=jnp.float32)
        for z in range(2):
            place = z * count
            for _, _, rows, target in slices:
                for n in range(blocks):
                    interp_ref[j, z, n, target : target + rows, :] = product[
                        place : place + rows, n * BLOCK : (n + 1) * BLOCK
                    ]
                place += rows
            for _, rows, _, scratch_row in windows:
                top = max(t + r for _, _, r, t in slices if t <= scratch_row + rows)
                if top < scratch_row + rows + 2:
                    interp_ref[j, z, :, top : top + 8, :] = jnp.zeros((blocks, 8, BLOCK), jnp.float32)

    scale = 1.0 / (length * total)
    lane = lax.broadcasted_iota(jnp.int32, (16, BLOCK), 1)
    row = lax.broadcasted_iota(jnp.int32, (16, BLOCK), 0)
    steps = []
    for j in range(2):
        rate = jnp.broadcast_to(rates_ref[0, j : j + 1, s : s + 1], (8, BLOCK))
        for n in range(blocks):
            range_idx = (lane[:8] + (n * BLOCK + 1)).astype(jnp.float32)
            steps.append(sin_cos(rate * (16.0 * range_idx) * scale))
    factors = [
        [jnp.broadcast_to(weights_ref[0, s, j : j + 1, a : a + 1], (16, BLOCK)) for a in range(4)]
        for j in range(2)
    ]

    for out_row, rows, beam, scratch_row in windows:
        start_tables = []
        beam_idx = (row + (first_beam + beam + 1)).astype(jnp.float32)
        for j in range(2):
            rate = jnp.broadcast_to(rates_ref[0, j : j + 1, s : s + 1], (16, BLOCK))
            for n in range(blocks):
                range_idx = (lane + (n * BLOCK + 1)).astype(jnp.float32)
                start_tables.append(sin_cos(rate * (beam_idx * range_idx) * scale))

        def step(i, tables, out_row=out_row, beam=beam, scratch_row=scratch_row):
            later = []
            if masked:
                at = row + (first_beam + beam + 16 * i)
                inside = (at >= 0) & (at < total)
            sums = [[None, None] for _ in range(blocks)]
            for j in range(2):
                for n in range(blocks):
                    sine, cosine = tables[j * blocks + n]
                    parts = []
                    for z in range(2):
                        acc = None
                        for a in range(4):
                            term = factors[j][a] * interp_ref[
                                j, z, n, pl.ds(scratch_row - 1 + a + 16 * i, 16), :
                            ]
                            acc = term if acc is None else acc + term
                        parts.append(acc)
                    real = cosine * parts[0] - sine * parts[1]
                    imag = sine * parts[0] + cosine * parts[1]
                    if j == 0:
                        sums[n] = [real, imag]
                    else:
                        sums[n] = [sums[n][0] + real, sums[n][1] + imag]
                    step_sine, step_cosine = steps[j * blocks + n]
                    step_sine = jnp.concatenate([step_sine, step_sine], axis=0)
                    step_cosine = jnp.concatenate([step_cosine, step_cosine], axis=0)
                    later.append(
                        (
                            sine * step_cosine + cosine * step_sine,
                            cosine * step_cosine - sine * step_sine,
                        )
                    )
            for n in range(blocks):
                for z in range(2):
                    value = sums[n][z]
                    if masked:
                        value = jnp.where(inside, value, 0.0)
                    target = out_row + 16 * i
                    if not isinstance(target, int):
                        target = pl.multiple_of(target, 16)
                    out_ref[z, pl.ds(target, 16), n * BLOCK : (n + 1) * BLOCK] = value.astype(
                        out_ref.dtype
                    )
            return later

        lax.fori_loop(0, rows // 16, step, start_tables, unroll=True)
        if partial:
            part = (slice(None), pl.ds(out_row, rows))
            send(out_ref.at[part], part)
    if partial:
        for copy in copies:
            copy.wait()


def merge(s, own, far, windows, out_rows, args, masked=False, edges=None, partial=0, after=(), kept=()):
    sector, total, weights, rates, bands = args
    length = own[0].shape[-1]
    placed_slices = []
    placed_windows = []
    base = 0
    for out_row, rows, beam, pieces in windows:
        lead = max(pieces, key=lambda item: item[2])[3] - beam
        low = min(item[3] for item in pieces) - beam
        origin = base + max(8, -low)
        origin += -(origin + lead) % 8
        top = origin + rows + 10
        for piece, first, count, at in pieces:
            placed_slices.append((piece, first, count, origin + at - beam))
            top = max(top, origin + at - beam + count)
        placed_windows.append((out_row, rows, beam, origin))
        base = -(-top // 8) * 8
    count = sum(item[2] for item in placed_slices)
    operands = [weights, rates, bands[s], *own, *far, *(edges or ())]
    operands.extend(item[0] for item in kept)
    operands.extend(after)
    kernel = functools.partial(
        merge_kernel,
        s,
        placed_slices,
        placed_windows,
        masked,
        sector,
        total,
        len(own),
        edges is not None,
        partial,
        [item[1:] for item in kept],
        len(after),
    )
    vmem = pl.BlockSpec(memory_space=pltpu.VMEM)
    out_shape = jax.ShapeDtypeStruct((2, out_rows, length), jnp.bfloat16)
    in_specs = [vmem] * len(operands)
    scratch = [
        pltpu.VMEM((2 * count, length), jnp.bfloat16),
        pltpu.VMEM((2, 2, length // BLOCK, base + 8, BLOCK), jnp.float32),
    ]
    if partial:
        scratch += [
            pltpu.VMEM((2, out_rows, length), jnp.bfloat16),
            pltpu.SemaphoreType.DMA((len(kept) + len(windows),)),
        ]
    anywhere = pl.BlockSpec(memory_space=pl.ANY)
    if after:
        in_specs[-len(after) :] = [anywhere] * len(after)
    return pl.pallas_call(
        kernel,
        out_shape=out_shape,
        in_specs=in_specs,
        out_specs=anywhere if partial else vmem,
        scratch_shapes=scratch,
        compiler_params=pltpu.CompilerParams(vmem_limit_bytes=VMEM_LIMIT),
        cost_estimate=MERGE_COST,
        name=f"merge{s}",
    )(*operands)


def to_sectors(x):
    subs, secs = lax.axis_size("sub"), lax.axis_size("sec")
    pairs = []
    for sub in range(subs):
        step = 1 if sub % 2 == 0 else -1
        for sec in range(secs):
            pairs.append((sub * secs + sec, sub * secs + (sec + step) % secs))
    return lax.ppermute(x, ("sub", "sec"), pairs)


def from_partner(x, bit):
    return lax.ppermute(x, "sub", [(i, i ^ 1 << bit) for i in range(lax.axis_size("sub"))])


def body(image, range_offsets, tap_weights, beam_weights, phase_rates):
    sector = image.shape[2]
    total = sector * lax.axis_size("sec")
    far = from_partner(image, 0)
    taps = jnp.swapaxes(tap_weights, 3, 4)
    rates = jnp.swapaxes(phase_rates, 1, 2)
    *bands, near = make_bands(range_offsets, taps, image)
    edges = jnp.concatenate([image[:, :, :EDGE], image[:, :, sector - EDGE :]], axis=2)
    near_edges = to_sectors(pack_edges(edges, from_partner(edges, 0)))
    (near_edges,) = relay((near_edges,), (bands[1], beam_weights, rates))
    args = (sector, total, beam_weights, rates, bands)

    mid1a = merge(
        0, [near], [far], [(0, 64, 30, [(0, 16, 80, 16)])], 64, args, after=(near_edges,)
    )
    (near_edges,) = relay((near_edges,), (mid1a,))
    swapped_edges = from_partner(near_edges, 0)
    mid1b = merge(0, [near], [far], [(0, 64, 94, [(0, 80, 80, 80)])], 64, args, after=(mid1a,))
    mid1c = merge(0, [near], [far], [(0, 64, 158, [(0, 144, 80, 144)])], 64, args, after=(mid1b,))
    ends1 = merge(
        0,
        [near],
        [far],
        [
            (0, 32, -2, [("low", 0, 16, -16), (0, 0, 32, 0)]),
            (32, 48, 212, [(0, 208, 48, 208), ("high", 0, 16, 256)]),
        ],
        80,
        args,
        masked=True,
        edges=(near_edges, swapped_edges),
        after=(mid1c,),
    )
    far_ends1 = from_partner(ends1, 1)
    far_mid1c = from_partner(mid1c, 1)
    far_mid1b = from_partner(mid1b, 1)
    far_mid1a = from_partner(mid1a, 1)
    mid2a = merge(
        1, [mid1a], [far_mid1a], [(0, 64, 31, [(0, 0, 64, 30)])], 64, args, after=(ends1,)
    )
    mid2b = merge(
        1,
        [mid1b, mid1a],
        [far_mid1b, far_mid1a],
        [(0, 64, 92, [(1, 48, 16, 78), (0, 0, 64, 94)])],
        64,
        args,
        after=(mid2a,),
    )
    mid2c = merge(
        1,
        [mid1c, mid1b],
        [far_mid1c, far_mid1b],
        [(0, 64, 156, [(1, 48, 16, 142), (0, 0, 64, 158)])],
        64,
        args,
        after=(mid2b,),
    )
    ends2 = merge(
        1,
        [ends1, mid1c, mid1a],
        [far_ends1, far_mid1c, far_mid1a],
        [
            (0, 32, -1, [(0, 0, 32, -2), (2, 0, 16, 30)]),
            (32, 48, 210, [(1, 48, 16, 206), (0, 32, 48, 212)]),
        ],
        80,
        args,
        masked=True,
        after=(mid2c,),
    )
    far_ends2 = from_partner(ends2, 2)
    far_mid2c = from_partner(mid2c, 2)
    far_mid2b = from_partner(mid2b, 2)
    far_mid2a = from_partner(mid2a, 2)
    part3a = merge(
        2, [mid2a], [far_mid2a], [(0, 48, 32, [(0, 0, 64, 31)])], 48, args, after=(ends2,)
    )
    part3b = merge(
        2,
        [mid2b, mid2a],
        [far_mid2b, far_mid2a],
        [(0, 64, 80, [(1, 48, 16, 79), (0, 0, 64, 92)])],
        64,
        args,
        after=(part3a,),
    )
    part3c = merge(
        2,
        [mid2c, mid2b],
        [far_mid2c, far_mid2b],
        [(0, 64, 144, [(1, 48, 16, 140), (0, 0, 64, 156)])],
        64,
        args,
        after=(part3b,),
    )
    merged = merge(
        2,
        [ends2, mid2c, mid2a],
        [far_ends2, far_mid2c, far_mid2a],
        [
            (0, 32, 0, [(0, 0, 32, -1), (2, 0, 16, 31)]),
            (208, 48, 208, [(1, 48, 16, 204), (0, 32, 48, 210)]),
        ],
        sector,
        args,
        partial=1,
        kept=[(part3a, 32, 48), (part3b, 80, 64), (part3c, 144, 64)],
    )
    return merged[None]


def solution(mesh):
    in_specs = (
        P("sub", None, "sec", None),
        P("sub", None, None, None),
        P("sub", None, None, None, None),
        P("sub", None, None, None),
        P("sub", None, None),
    )
    out_specs = P("sub", None, "sec", None)
    return jax.shard_map(body, mesh=mesh, in_specs=in_specs, out_specs=out_specs, check_vma=False)
```

```python
import functools
import math
import jax
import jax.numpy as jnp
from jax import lax
from jax.experimental import pallas as pl
from jax.experimental.pallas import tpu as pltpu
from jax.sharding import PartitionSpec as P

SECTIONS = 3
BLOCK = 128
TAPS = 8
MARGIN_ROWS = 12
VMEM_LIMIT = 40 * 1024 * 1024
MERGE_COST = pl.CostEstimate(flops=800_000_000, bytes_accessed=1000, transcendentals=0)
SMALL_COST = pl.CostEstimate(flops=1000, bytes_accessed=1000, transcendentals=0)


def sin_cos(angle):
    quadrant = jnp.floor(angle * (2.0 / math.pi) + 0.5)
    rest = angle - quadrant * 1.5703125
    rest = rest - quadrant * 4.8375129699707031e-4
    rest = rest - quadrant * 7.5495690e-8
    square = rest * rest
    sine = rest + rest * square * (
        -1.6666654611e-1 + square * (8.3321608736e-3 - square * 1.9515295891e-4)
    )
    cosine = 1.0 - 0.5 * square + square * square * (
        4.166664568298827e-2 + square * (-1.388731625493765e-3 + square * 2.443315711809948e-5)
    )
    turn = quadrant.astype(jnp.int32)
    odd = (turn & 1) == 1
    sin_value = jnp.where(odd, cosine, sine)
    cos_value = jnp.where(odd, sine, cosine)
    sin_value = jnp.where((turn & 2) == 2, -sin_value, sin_value)
    cos_value = jnp.where(((turn + 1) & 2) == 2, -cos_value, cos_value)
    return sin_value, cos_value


def band_kernel(offsets_ref, taps_ref, image_ref, *out_refs):
    out_refs[-1][...] = image_ref[...]
    blocks = offsets_ref.shape[3]
    length = blocks * BLOCK
    row = lax.broadcasted_iota(jnp.int32, (16, BLOCK), 0)
    lane = lax.broadcasted_iota(jnp.int32, (16, BLOCK), 1)
    diff = row - lane
    for s, out_ref in enumerate(out_refs[:-1]):
        out_ref[...] = jnp.zeros(out_ref.shape, out_ref.dtype)
        for j in range(2):
            taps = taps_ref[0, s, j].astype(jnp.float32)
            for n in range(blocks):
                base = offsets_ref[0, s, j, n] - MARGIN_ROWS
                for first in range(-16, BLOCK + 16, 16):
                    place = n * BLOCK + first
                    if place < 0 or place >= length:
                        continue
                    shift = diff + (first - base)
                    value = jnp.zeros((16, BLOCK), jnp.float32)
                    for t in range(TAPS):
                        value = jnp.where(shift == t, taps[t : t + 1, :], value)
                    out_ref[j, place : place + 16, n * BLOCK : (n + 1) * BLOCK] = value.astype(
                        out_ref.dtype
                    )


def make_bands(range_offsets, taps, image):
    length = image.shape[3]
    vmem = pl.BlockSpec(memory_space=pltpu.VMEM)
    return pl.pallas_call(
        band_kernel,
        out_shape=[jax.ShapeDtypeStruct((2, length, length), jnp.bfloat16)] * SECTIONS
        + [jax.ShapeDtypeStruct(image.shape, image.dtype)],
        in_specs=[pl.BlockSpec(memory_space=pltpu.SMEM), vmem, vmem],
        out_specs=[vmem] * (SECTIONS + 1),
        compiler_params=pltpu.CompilerParams(vmem_limit_bytes=VMEM_LIMIT),
        cost_estimate=SMALL_COST,
        name="bands",
    )(range_offsets, taps, image)


EDGE = 8


def pack_kernel(near_ref, far_ref, out_ref):
    even = lax.rem(lax.axis_index("sub"), 2) == 0
    for j, ref in enumerate((near_ref, far_ref)):
        for z in range(2):
            rows = ref[0, z].astype(jnp.float32)
            rows = jnp.where(even, rows[EDGE:], rows[:EDGE])
            out_ref[j, z] = rows.astype(out_ref.dtype)


def pack_edges(near, far):
    vmem = pl.BlockSpec(memory_space=pltpu.VMEM)
    return pl.pallas_call(
        pack_kernel,
        out_shape=jax.ShapeDtypeStruct((2, 2, EDGE, near.shape[3]), near.dtype),
        in_specs=[vmem] * 2,
        out_specs=vmem,
        compiler_params=pltpu.CompilerParams(vmem_limit_bytes=VMEM_LIMIT),
        cost_estimate=SMALL_COST,
        name="pack",
    )(near, far)


def relay_kernel(count, *refs):
    for source, target in zip(refs[:count], refs[-count:]):
        target[...] = source[...]


def relay(arrays, after):
    vmem = pl.BlockSpec(memory_space=pltpu.VMEM)
    return pl.pallas_call(
        functools.partial(relay_kernel, len(arrays)),
        out_shape=[jax.ShapeDtypeStruct(x.shape, x.dtype) for x in arrays],
        in_specs=[vmem] * len(arrays) + [pl.BlockSpec(memory_space=pl.ANY)] * len(after),
        out_specs=[vmem] * len(arrays),
        compiler_params=pltpu.CompilerParams(vmem_limit_bytes=VMEM_LIMIT),
        cost_estimate=SMALL_COST,
        name="relay",
    )(*arrays, *after)


def rows_of(ref, z, first, rows):
    return ref[(0,) * (len(ref.shape) - 3) + (z, slice(first, first + rows))]


def merge_kernel(s, slices, windows, masked, sector, total, pieces, edges, partial, kept, unread, *refs):
    weights_ref, rates_ref, bands_ref = refs[:3]
    own_refs = refs[3 : 3 + pieces]
    far_refs = refs[3 + pieces : 3 + 2 * pieces]
    rest = refs[3 + 2 * pieces :]
    if edges:
        near_edges_ref, swapped_edges_ref, *rest = rest
    kept_refs, rest = rest[: len(kept)], rest[len(kept) + unread :]
    out_ref, rows_ref, interp_ref, *rest = rest
    if partial:
        hbm_ref, (out_ref, sems) = out_ref, rest
        copies = []

        def send(source, part):
            copies.append(pltpu.make_async_copy(source, hbm_ref.at[part], sems.at[len(copies)]))
            copies[-1].start()

        for ref, (first, rows) in zip(kept_refs, kept):
            send(ref, (slice(None), pl.ds(first, rows)))
    length = bands_ref.shape[1]
    blocks = length // BLOCK
    count = sum(item[2] for item in slices)
    place_in_sec = lax.axis_index("sec")
    first_beam = place_in_sec * sector
    even = lax.rem(lax.axis_index("sub"), 2) == 0

    for j, piece_refs in enumerate((own_refs, far_refs)):
        for z in range(2):
            place = z * count
            for piece, first, rows, _ in slices:
                if piece in ("low", "high"):
                    low = piece == "low"
                    near = even if low else jnp.logical_not(even)
                    end = 0 if low else lax.axis_size("sec") - 1
                    inner = place_in_sec != end
                    target = slice(place, place + rows)

                    def put(ref, child, z=z, low=low, target=target):
                        beams = ref[child, z].astype(jnp.float32)
                        blank = jnp.zeros_like(beams)
                        both = [blank, beams] if low else [beams, blank]
                        rows_ref[target, :] = jnp.concatenate(both, axis=0).astype(rows_ref.dtype)

                    @pl.when(jnp.logical_and(inner, near))
                    def _(put=put, j=j):
                        put(near_edges_ref, j)

                    @pl.when(jnp.logical_and(inner, jnp.logical_not(near)))
                    def _(put=put, j=j):
                        put(swapped_edges_ref, 1 - j)

                    @pl.when(jnp.logical_not(inner))
                    def _(target=target, rows=rows):
                        rows_ref[target, :] = jnp.zeros((rows, length), rows_ref.dtype)

                else:
                    rows_ref[place : place + rows, :] = rows_of(piece_refs[piece], z, first, rows)
                place += rows
        product = jnp.dot(rows_ref[...], bands_ref[j], preferred_element_type=jnp.float32)
        for z in range(2):
            place = z * count
            for _, _, rows, target in slices:
                for n in range(blocks):
                    interp_ref[j, z, n, target : target + rows, :] = product[
                        place : place + rows, n * BLOCK : (n + 1) * BLOCK
                    ]
                place += rows
            for _, rows, _, scratch_row in windows:
                top = max(t + r for _, _, r, t in slices if t <= scratch_row + rows)
                if top < scratch_row + rows + 2:
                    interp_ref[j, z, :, top : top + 8, :] = jnp.zeros((blocks, 8, BLOCK), jnp.float32)

    scale = 1.0 / (length * total)
    lane = lax.broadcasted_iota(jnp.int32, (16, BLOCK), 1)
    row = lax.broadcasted_iota(jnp.int32, (16, BLOCK), 0)
    steps = []
    for j in range(2):
        rate = jnp.broadcast_to(rates_ref[0, j : j + 1, s : s + 1], (8, BLOCK))
        for n in range(blocks):
            range_idx = (lane[:8] + (n * BLOCK + 1)).astype(jnp.float32)
            steps.append(sin_cos(rate * (16.0 * range_idx) * scale))
    factors = [
        [jnp.broadcast_to(weights_ref[0, s, j : j + 1, a : a + 1], (16, BLOCK)) for a in range(4)]
        for j in range(2)
    ]

    for out_row, rows, beam, scratch_row in windows:
        start_tables = []
        beam_idx = (row + (first_beam + beam + 1)).astype(jnp.float32)
        for j in range(2):
            rate = jnp.broadcast_to(rates_ref[0, j : j + 1, s : s + 1], (16, BLOCK))
            for n in range(blocks):
                range_idx = (lane + (n * BLOCK + 1)).astype(jnp.float32)
                start_tables.append(sin_cos(rate * (beam_idx * range_idx) * scale))

        def step(i, tables, out_row=out_row, beam=beam, scratch_row=scratch_row):
            later = []
            if masked:
                at = row + (first_beam + beam + 16 * i)
                inside = (at >= 0) & (at < total)
            sums = [[None, None] for _ in range(blocks)]
            for j in range(2):
                for n in range(blocks):
                    sine, cosine = tables[j * blocks + n]
                    parts = []
                    for z in range(2):
                        acc = None
                        for a in range(4):
                            term = factors[j][a] * interp_ref[
                                j, z, n, pl.ds(scratch_row - 1 + a + 16 * i, 16), :
                            ]
                            acc = term if acc is None else acc + term
                        parts.append(acc)
                    real = cosine * parts[0] - sine * parts[1]
                    imag = sine * parts[0] + cosine * parts[1]
                    if j == 0:
                        sums[n] = [real, imag]
                    else:
                        sums[n] = [sums[n][0] + real, sums[n][1] + imag]
                    step_sine, step_cosine = steps[j * blocks + n]
                    step_sine = jnp.concatenate([step_sine, step_sine], axis=0)
                    step_cosine = jnp.concatenate([step_cosine, step_cosine], axis=0)
                    later.append(
                        (
                            sine * step_cosine + cosine * step_sine,
                            cosine * step_cosine - sine * step_sine,
                        )
                    )
            for n in range(blocks):
                for z in range(2):
                    value = sums[n][z]
                    if masked:
                        value = jnp.where(inside, value, 0.0)
                    target = out_row + 16 * i
                    if not isinstance(target, int):
                        target = pl.multiple_of(target, 16)
                    out_ref[z, pl.ds(target, 16), n * BLOCK : (n + 1) * BLOCK] = value.astype(
                        out_ref.dtype
                    )
            return later

        lax.fori_loop(0, rows // 16, step, start_tables, unroll=True)
        if partial:
            part = (slice(None), pl.ds(out_row, rows))
            send(out_ref.at[part], part)
    if partial:
        for copy in copies:
            copy.wait()


def merge(s, own, far, windows, out_rows, args, masked=False, edges=None, partial=0, after=(), kept=()):
    sector, total, weights, rates, bands = args
    length = own[0].shape[-1]
    placed_slices = []
    placed_windows = []
    base = 0
    for out_row, rows, beam, pieces in windows:
        lead = max(pieces, key=lambda item: item[2])[3] - beam
        low = min(item[3] for item in pieces) - beam
        origin = base + max(8, -low)
        origin += -(origin + lead) % 8
        top = origin + rows + 10
        for piece, first, count, at in pieces:
            placed_slices.append((piece, first, count, origin + at - beam))
            top = max(top, origin + at - beam + count)
        placed_windows.append((out_row, rows, beam, origin))
        base = -(-top // 8) * 8
    count = sum(item[2] for item in placed_slices)
    operands = [weights, rates, bands[s], *own, *far, *(edges or ())]
    operands.extend(item[0] for item in kept)
    operands.extend(after)
    kernel = functools.partial(
        merge_kernel,
        s,
        placed_slices,
        placed_windows,
        masked,
        sector,
        total,
        len(own),
        edges is not None,
        partial,
        [item[1:] for item in kept],
        len(after),
    )
    vmem = pl.BlockSpec(memory_space=pltpu.VMEM)
    out_shape = jax.ShapeDtypeStruct((2, out_rows, length), jnp.bfloat16)
    in_specs = [vmem] * len(operands)
    scratch = [
        pltpu.VMEM((2 * count, length), jnp.bfloat16),
        pltpu.VMEM((2, 2, length // BLOCK, base + 8, BLOCK), jnp.float32),
    ]
    if partial:
        scratch += [
            pltpu.VMEM((2, out_rows, length), jnp.bfloat16),
            pltpu.SemaphoreType.DMA((len(kept) + len(windows),)),
        ]
    anywhere = pl.BlockSpec(memory_space=pl.ANY)
    if after:
        in_specs[-len(after) :] = [anywhere] * len(after)
    return pl.pallas_call(
        kernel,
        out_shape=out_shape,
        in_specs=in_specs,
        out_specs=anywhere if partial else vmem,
        scratch_shapes=scratch,
        compiler_params=pltpu.CompilerParams(vmem_limit_bytes=VMEM_LIMIT),
        cost_estimate=MERGE_COST,
        name=f"merge{s}",
    )(*operands)


def to_sectors(x):
    subs, secs = lax.axis_size("sub"), lax.axis_size("sec")
    pairs = []
    for sub in range(subs):
        step = 1 if sub % 2 == 0 else -1
        for sec in range(secs):
            pairs.append((sub * secs + sec, sub * secs + (sec + step) % secs))
    return lax.ppermute(x, ("sub", "sec"), pairs)


def from_partner(x, bit):
    return lax.ppermute(x, "sub", [(i, i ^ 1 << bit) for i in range(lax.axis_size("sub"))])


def body(image, range_offsets, tap_weights, beam_weights, phase_rates):
    sector = image.shape[2]
    total = sector * lax.axis_size("sec")
    far = from_partner(image, 0)
    taps = jnp.swapaxes(tap_weights, 3, 4)
    rates = jnp.swapaxes(phase_rates, 1, 2)
    *bands, near = make_bands(range_offsets, taps, image)
    edges = jnp.concatenate([image[:, :, :EDGE], image[:, :, sector - EDGE :]], axis=2)
    near_edges = to_sectors(pack_edges(edges, from_partner(edges, 0)))
    (near_edges,) = relay((near_edges,), (bands[1], beam_weights, rates))
    args = (sector, total, beam_weights, rates, bands)

    mid1a = merge(
        0, [near], [far], [(0, 80, 30, [(0, 16, 96, 16)])], 80, args, after=(near_edges,)
    )
    (near_edges,) = relay((near_edges,), (mid1a,))
    swapped_edges = from_partner(near_edges, 0)
    mid1b = merge(
        0, [near], [far], [(0, 112, 110, [(0, 96, 128, 96)])], 112, args, after=(mid1a,)
    )
    ends1 = merge(
        0,
        [near],
        [far],
        [
            (0, 32, -2, [("low", 0, 16, -16), (0, 0, 32, 0)]),
            (32, 48, 212, [(0, 208, 48, 208), ("high", 0, 16, 256)]),
        ],
        80,
        args,
        masked=True,
        edges=(near_edges, swapped_edges),
        after=(mid1b,),
    )
    far_ends1 = from_partner(ends1, 1)
    far_mid1b = from_partner(mid1b, 1)
    far_mid1a = from_partner(mid1a, 1)
    mid2a = merge(
        1, [mid1a], [far_mid1a], [(0, 80, 31, [(0, 0, 80, 30)])], 80, args, after=(ends1,)
    )
    mid2b = merge(
        1,
        [mid1b, mid1a],
        [far_mid1b, far_mid1a],
        [(0, 112, 108, [(1, 64, 16, 94), (0, 0, 112, 110)])],
        112,
        args,
        after=(mid2a,),
    )
    ends2 = merge(
        1,
        [ends1, mid1b, mid1a],
        [far_ends1, far_mid1b, far_mid1a],
        [
            (0, 32, -1, [(0, 0, 32, -2), (2, 0, 16, 30)]),
            (32, 48, 210, [(1, 96, 16, 206), (0, 32, 48, 212)]),
        ],
        80,
        args,
        masked=True,
        after=(mid2b,),
    )
    far_ends2 = from_partner(ends2, 2)
    far_mid2b = from_partner(mid2b, 2)
    far_mid2a = from_partner(mid2a, 2)
    part3a = merge(
        2, [mid2a], [far_mid2a], [(0, 64, 32, [(0, 0, 80, 31)])], 64, args, after=(ends2,)
    )
    part3b = merge(
        2,
        [mid2b, mid2a],
        [far_mid2b, far_mid2a],
        [(0, 112, 96, [(1, 64, 16, 95), (0, 0, 112, 108)])],
        112,
        args,
        after=(part3a,),
    )
    merged = merge(
        2,
        [ends2, mid2b, mid2a],
        [far_ends2, far_mid2b, far_mid2a],
        [
            (0, 32, 0, [(0, 0, 32, -1), (2, 0, 16, 31)]),
            (208, 48, 208, [(1, 96, 16, 204), (0, 32, 48, 210)]),
        ],
        sector,
        args,
        partial=1,
        kept=[(part3a, 32, 64), (part3b, 96, 112)],
    )
    return merged[None]


def solution(mesh):
    in_specs = (
        P("sub", None, "sec", None),
        P("sub", None, None, None),
        P("sub", None, None, None, None),
        P("sub", None, None, None),
        P("sub", None, None),
    )
    out_specs = P("sub", None, "sec", None)
    return jax.shard_map(body, mesh=mesh, in_specs=in_specs, out_specs=out_specs, check_vma=False)
```

```python
import functools
import math
import jax
import jax.numpy as jnp
from jax import lax
from jax.experimental import pallas as pl
from jax.experimental.pallas import tpu as pltpu
from jax.sharding import PartitionSpec as P

SECTIONS = 3
BLOCK = 128
TAPS = 8
MARGIN_ROWS = 12
VMEM_LIMIT = 40 * 1024 * 1024
MERGE_COST = pl.CostEstimate(flops=800_000_000, bytes_accessed=1000, transcendentals=0)
SMALL_COST = pl.CostEstimate(flops=1000, bytes_accessed=1000, transcendentals=0)


def sin_cos(angle):
    quadrant = jnp.floor(angle * (2.0 / math.pi) + 0.5)
    rest = angle - quadrant * 1.5703125
    rest = rest - quadrant * 4.8375129699707031e-4
    rest = rest - quadrant * 7.5495690e-8
    square = rest * rest
    sine = rest + rest * square * (
        -1.6666654611e-1 + square * (8.3321608736e-3 - square * 1.9515295891e-4)
    )
    cosine = 1.0 - 0.5 * square + square * square * (
        4.166664568298827e-2 + square * (-1.388731625493765e-3 + square * 2.443315711809948e-5)
    )
    turn = quadrant.astype(jnp.int32)
    odd = (turn & 1) == 1
    sin_value = jnp.where(odd, cosine, sine)
    cos_value = jnp.where(odd, sine, cosine)
    sin_value = jnp.where((turn & 2) == 2, -sin_value, sin_value)
    cos_value = jnp.where(((turn + 1) & 2) == 2, -cos_value, cos_value)
    return sin_value, cos_value


def band_kernel(offsets_ref, taps_ref, image_ref, *out_refs):
    out_refs[-1][...] = image_ref[...]
    blocks = offsets_ref.shape[3]
    length = blocks * BLOCK
    row = lax.broadcasted_iota(jnp.int32, (16, BLOCK), 0)
    lane = lax.broadcasted_iota(jnp.int32, (16, BLOCK), 1)
    diff = row - lane
    for s, out_ref in enumerate(out_refs[:-1]):
        out_ref[...] = jnp.zeros(out_ref.shape, out_ref.dtype)
        for j in range(2):
            taps = taps_ref[0, s, j].astype(jnp.float32)
            for n in range(blocks):
                base = offsets_ref[0, s, j, n] - MARGIN_ROWS
                for first in range(-16, BLOCK + 16, 16):
                    place = n * BLOCK + first
                    if place < 0 or place >= length:
                        continue
                    shift = diff + (first - base)
                    value = jnp.zeros((16, BLOCK), jnp.float32)
                    for t in range(TAPS):
                        value = jnp.where(shift == t, taps[t : t + 1, :], value)
                    out_ref[j, place : place + 16, n * BLOCK : (n + 1) * BLOCK] = value.astype(
                        out_ref.dtype
                    )


def make_bands(range_offsets, taps, image):
    length = image.shape[3]
    vmem = pl.BlockSpec(memory_space=pltpu.VMEM)
    return pl.pallas_call(
        band_kernel,
        out_shape=[jax.ShapeDtypeStruct((2, length, length), jnp.bfloat16)] * SECTIONS
        + [jax.ShapeDtypeStruct(image.shape, image.dtype)],
        in_specs=[pl.BlockSpec(memory_space=pltpu.SMEM), vmem, vmem],
        out_specs=[vmem] * (SECTIONS + 1),
        compiler_params=pltpu.CompilerParams(vmem_limit_bytes=VMEM_LIMIT),
        cost_estimate=SMALL_COST,
        name="bands",
    )(range_offsets, taps, image)


EDGE = 8


def pack_kernel(near_ref, far_ref, out_ref):
    even = lax.rem(lax.axis_index("sub"), 2) == 0
    for j, ref in enumerate((near_ref, far_ref)):
        for z in range(2):
            rows = ref[0, z].astype(jnp.float32)
            rows = jnp.where(even, rows[EDGE:], rows[:EDGE])
            out_ref[j, z] = rows.astype(out_ref.dtype)


def pack_edges(near, far):
    vmem = pl.BlockSpec(memory_space=pltpu.VMEM)
    return pl.pallas_call(
        pack_kernel,
        out_shape=jax.ShapeDtypeStruct((2, 2, EDGE, near.shape[3]), near.dtype),
        in_specs=[vmem] * 2,
        out_specs=vmem,
        compiler_params=pltpu.CompilerParams(vmem_limit_bytes=VMEM_LIMIT),
        cost_estimate=SMALL_COST,
        name="pack",
    )(near, far)


def relay_kernel(count, *refs):
    for source, target in zip(refs[:count], refs[-count:]):
        target[...] = source[...]


def relay(arrays, after):
    vmem = pl.BlockSpec(memory_space=pltpu.VMEM)
    return pl.pallas_call(
        functools.partial(relay_kernel, len(arrays)),
        out_shape=[jax.ShapeDtypeStruct(x.shape, x.dtype) for x in arrays],
        in_specs=[vmem] * len(arrays) + [pl.BlockSpec(memory_space=pl.ANY)] * len(after),
        out_specs=[vmem] * len(arrays),
        compiler_params=pltpu.CompilerParams(vmem_limit_bytes=VMEM_LIMIT),
        cost_estimate=SMALL_COST,
        name="relay",
    )(*arrays, *after)


def rows_of(ref, z, first, rows):
    return ref[(0,) * (len(ref.shape) - 3) + (z, slice(first, first + rows))]


def merge_kernel(s, slices, windows, masked, sector, total, pieces, edges, partial, kept, unread, *refs):
    weights_ref, rates_ref, bands_ref = refs[:3]
    own_refs = refs[3 : 3 + pieces]
    far_refs = refs[3 + pieces : 3 + 2 * pieces]
    rest = refs[3 + 2 * pieces :]
    if edges:
        near_edges_ref, swapped_edges_ref, *rest = rest
    kept_refs, rest = rest[: len(kept)], rest[len(kept) + unread :]
    out_ref, rows_ref, interp_ref, *rest = rest
    if partial:
        hbm_ref, (out_ref, sems) = out_ref, rest
        copies = []

        def send(source, part):
            copies.append(pltpu.make_async_copy(source, hbm_ref.at[part], sems.at[len(copies)]))
            copies[-1].start()

        for ref, (first, rows) in zip(kept_refs, kept):
            send(ref, (slice(None), pl.ds(first, rows)))
    length = bands_ref.shape[1]
    blocks = length // BLOCK
    count = sum(item[2] for item in slices)
    place_in_sec = lax.axis_index("sec")
    first_beam = place_in_sec * sector
    even = lax.rem(lax.axis_index("sub"), 2) == 0

    for j, piece_refs in enumerate((own_refs, far_refs)):
        for z in range(2):
            place = z * count
            for piece, first, rows, _ in slices:
                if piece in ("low", "high"):
                    low = piece == "low"
                    near = even if low else jnp.logical_not(even)
                    end = 0 if low else lax.axis_size("sec") - 1
                    inner = place_in_sec != end
                    target = slice(place, place + rows)

                    def put(ref, child, z=z, low=low, target=target):
                        beams = ref[child, z].astype(jnp.float32)
                        blank = jnp.zeros_like(beams)
                        both = [blank, beams] if low else [beams, blank]
                        rows_ref[target, :] = jnp.concatenate(both, axis=0).astype(rows_ref.dtype)

                    @pl.when(jnp.logical_and(inner, near))
                    def _(put=put, j=j):
                        put(near_edges_ref, j)

                    @pl.when(jnp.logical_and(inner, jnp.logical_not(near)))
                    def _(put=put, j=j):
                        put(swapped_edges_ref, 1 - j)

                    @pl.when(jnp.logical_not(inner))
                    def _(target=target, rows=rows):
                        rows_ref[target, :] = jnp.zeros((rows, length), rows_ref.dtype)

                else:
                    rows_ref[place : place + rows, :] = rows_of(piece_refs[piece], z, first, rows)
                place += rows
        product = jnp.dot(rows_ref[...], bands_ref[j], preferred_element_type=jnp.float32)
        for z in range(2):
            place = z * count
            for _, _, rows, target in slices:
                for n in range(blocks):
                    interp_ref[j, z, n, target : target + rows, :] = product[
                        place : place + rows, n * BLOCK : (n + 1) * BLOCK
                    ]
                place += rows
            for _, rows, _, scratch_row in windows:
                top = max(t + r for _, _, r, t in slices if t <= scratch_row + rows)
                if top < scratch_row + rows + 2:
                    interp_ref[j, z, :, top : top + 8, :] = jnp.zeros((blocks, 8, BLOCK), jnp.float32)

    scale = 1.0 / (length * total)
    lane = lax.broadcasted_iota(jnp.int32, (16, BLOCK), 1)
    row = lax.broadcasted_iota(jnp.int32, (16, BLOCK), 0)
    steps = []
    for j in range(2):
        rate = jnp.broadcast_to(rates_ref[0, j : j + 1, s : s + 1], (8, BLOCK))
        for n in range(blocks):
            range_idx = (lane[:8] + (n * BLOCK + 1)).astype(jnp.float32)
            steps.append(sin_cos(rate * (16.0 * range_idx) * scale))
    factors = [
        [jnp.broadcast_to(weights_ref[0, s, j : j + 1, a : a + 1], (16, BLOCK)) for a in range(4)]
        for j in range(2)
    ]

    for out_row, rows, beam, scratch_row in windows:
        start_tables = []
        beam_idx = (row + (first_beam + beam + 1)).astype(jnp.float32)
        for j in range(2):
            rate = jnp.broadcast_to(rates_ref[0, j : j + 1, s : s + 1], (16, BLOCK))
            for n in range(blocks):
                range_idx = (lane + (n * BLOCK + 1)).astype(jnp.float32)
                start_tables.append(sin_cos(rate * (beam_idx * range_idx) * scale))

        def step(i, tables, out_row=out_row, beam=beam, scratch_row=scratch_row):
            later = []
            if masked:
                at = row + (first_beam + beam + 16 * i)
                inside = (at >= 0) & (at < total)
            sums = [[None, None] for _ in range(blocks)]
            for j in range(2):
                for n in range(blocks):
                    sine, cosine = tables[j * blocks + n]
                    parts = []
                    for z in range(2):
                        acc = None
                        for a in range(4):
                            term = factors[j][a] * interp_ref[
                                j, z, n, pl.ds(scratch_row - 1 + a + 16 * i, 16), :
                            ]
                            acc = term if acc is None else acc + term
                        parts.append(acc)
                    real = cosine * parts[0] - sine * parts[1]
                    imag = sine * parts[0] + cosine * parts[1]
                    if j == 0:
                        sums[n] = [real, imag]
                    else:
                        sums[n] = [sums[n][0] + real, sums[n][1] + imag]
                    step_sine, step_cosine = steps[j * blocks + n]
                    step_sine = jnp.concatenate([step_sine, step_sine], axis=0)
                    step_cosine = jnp.concatenate([step_cosine, step_cosine], axis=0)
                    later.append(
                        (
                            sine * step_cosine + cosine * step_sine,
                            cosine * step_cosine - sine * step_sine,
                        )
                    )
            for n in range(blocks):
                for z in range(2):
                    value = sums[n][z]
                    if masked:
                        value = jnp.where(inside, value, 0.0)
                    target = out_row + 16 * i
                    if not isinstance(target, int):
                        target = pl.multiple_of(target, 16)
                    out_ref[z, pl.ds(target, 16), n * BLOCK : (n + 1) * BLOCK] = value.astype(
                        out_ref.dtype
                    )
            return later

        lax.fori_loop(0, rows // 16, step, start_tables, unroll=True)
        if partial:
            part = (slice(None), pl.ds(out_row, rows))
            send(out_ref.at[part], part)
    if partial:
        for copy in copies:
            copy.wait()


def merge(s, own, far, windows, out_rows, args, masked=False, edges=None, partial=0, after=(), kept=()):
    sector, total, weights, rates, bands = args
    length = own[0].shape[-1]
    placed_slices = []
    placed_windows = []
    base = 0
    for out_row, rows, beam, pieces in windows:
        lead = max(pieces, key=lambda item: item[2])[3] - beam
        low = min(item[3] for item in pieces) - beam
        origin = base + max(8, -low)
        origin += -(origin + lead) % 8
        top = origin + rows + 10
        for piece, first, count, at in pieces:
            placed_slices.append((piece, first, count, origin + at - beam))
            top = max(top, origin + at - beam + count)
        placed_windows.append((out_row, rows, beam, origin))
        base = -(-top // 8) * 8
    count = sum(item[2] for item in placed_slices)
    operands = [weights, rates, bands[s], *own, *far, *(edges or ())]
    operands.extend(item[0] for item in kept)
    operands.extend(after)
    kernel = functools.partial(
        merge_kernel,
        s,
        placed_slices,
        placed_windows,
        masked,
        sector,
        total,
        len(own),
        edges is not None,
        partial,
        [item[1:] for item in kept],
        len(after),
    )
    vmem = pl.BlockSpec(memory_space=pltpu.VMEM)
    out_shape = jax.ShapeDtypeStruct((2, out_rows, length), jnp.bfloat16)
    in_specs = [vmem] * len(operands)
    scratch = [
        pltpu.VMEM((2 * count, length), jnp.bfloat16),
        pltpu.VMEM((2, 2, length // BLOCK, base + 8, BLOCK), jnp.float32),
    ]
    if partial:
        scratch += [
            pltpu.VMEM((2, out_rows, length), jnp.bfloat16),
            pltpu.SemaphoreType.DMA((len(kept) + len(windows),)),
        ]
    anywhere = pl.BlockSpec(memory_space=pl.ANY)
    if after:
        in_specs[-len(after) :] = [anywhere] * len(after)
    return pl.pallas_call(
        kernel,
        out_shape=out_shape,
        in_specs=in_specs,
        out_specs=anywhere if partial else vmem,
        scratch_shapes=scratch,
        compiler_params=pltpu.CompilerParams(vmem_limit_bytes=VMEM_LIMIT),
        cost_estimate=MERGE_COST,
        name=f"merge{s}",
    )(*operands)


def to_sectors(x):
    subs, secs = lax.axis_size("sub"), lax.axis_size("sec")
    pairs = []
    for sub in range(subs):
        step = 1 if sub % 2 == 0 else -1
        for sec in range(secs):
            pairs.append((sub * secs + sec, sub * secs + (sec + step) % secs))
    return lax.ppermute(x, ("sub", "sec"), pairs)


def from_partner(x, bit):
    return lax.ppermute(x, "sub", [(i, i ^ 1 << bit) for i in range(lax.axis_size("sub"))])


def body(image, range_offsets, tap_weights, beam_weights, phase_rates):
    sector = image.shape[2]
    total = sector * lax.axis_size("sec")
    far = from_partner(image, 0)
    taps = jnp.swapaxes(tap_weights, 3, 4)
    rates = jnp.swapaxes(phase_rates, 1, 2)
    *bands, near = make_bands(range_offsets, taps, image)
    edges = jnp.concatenate([image[:, :, :EDGE], image[:, :, sector - EDGE :]], axis=2)
    near_edges = to_sectors(pack_edges(edges, from_partner(edges, 0)))
    (near_edges,) = relay((near_edges,), (bands[1], beam_weights, rates))
    args = (sector, total, beam_weights, rates, bands)

    mid1a = merge(
        0, [near], [far], [(0, 64, 30, [(0, 16, 80, 16)])], 64, args, after=(near_edges,)
    )
    (near_edges,) = relay((near_edges,), (mid1a,))
    swapped_edges = from_partner(near_edges, 0)
    mid1b = merge(0, [near], [far], [(0, 64, 94, [(0, 80, 80, 80)])], 64, args, after=(mid1a,))
    mid1c = merge(0, [near], [far], [(0, 80, 158, [(0, 144, 96, 144)])], 80, args, after=(mid1b,))
    ends1 = merge(
        0,
        [near],
        [far],
        [
            (0, 32, -2, [("low", 0, 16, -16), (0, 0, 32, 0)]),
            (32, 32, 228, [(0, 224, 32, 224), ("high", 0, 16, 256)]),
        ],
        64,
        args,
        masked=True,
        edges=(near_edges, swapped_edges),
        after=(mid1c,),
    )
    far_ends1 = from_partner(ends1, 1)
    far_mid1c = from_partner(mid1c, 1)
    far_mid1b = from_partner(mid1b, 1)
    far_mid1a = from_partner(mid1a, 1)
    mid2a = merge(
        1, [mid1a], [far_mid1a], [(0, 64, 31, [(0, 0, 64, 30)])], 64, args, after=(ends1,)
    )
    mid2b = merge(
        1,
        [mid1b, mid1a],
        [far_mid1b, far_mid1a],
        [(0, 64, 92, [(1, 48, 16, 78), (0, 0, 64, 94)])],
        64,
        args,
        after=(mid2a,),
    )
    mid2c = merge(
        1,
        [mid1c, mid1b],
        [far_mid1c, far_mid1b],
        [(0, 80, 156, [(1, 48, 16, 142), (0, 0, 80, 158)])],
        80,
        args,
        after=(mid2b,),
    )
    ends2 = merge(
        1,
        [ends1, mid1c, mid1a],
        [far_ends1, far_mid1c, far_mid1a],
        [
            (0, 32, -1, [(0, 0, 32, -2), (2, 0, 16, 30)]),
            (32, 32, 226, [(1, 64, 16, 222), (0, 32, 32, 228)]),
        ],
        64,
        args,
        masked=True,
        after=(mid2c,),
    )
    far_ends2 = from_partner(ends2, 2)
    far_mid2c = from_partner(mid2c, 2)
    far_mid2b = from_partner(mid2b, 2)
    far_mid2a = from_partner(mid2a, 2)
    part3a = merge(
        2, [mid2a], [far_mid2a], [(0, 48, 32, [(0, 0, 64, 31)])], 48, args, after=(ends2,)
    )
    part3b = merge(
        2,
        [mid2b, mid2a],
        [far_mid2b, far_mid2a],
        [(0, 64, 80, [(1, 48, 16, 79), (0, 0, 64, 92)])],
        64,
        args,
        after=(part3a,),
    )
    part3c = merge(
        2,
        [mid2c, mid2b],
        [far_mid2c, far_mid2b],
        [(0, 80, 144, [(1, 48, 16, 140), (0, 0, 80, 156)])],
        80,
        args,
        after=(part3b,),
    )
    merged = merge(
        2,
        [ends2, mid2c, mid2a],
        [far_ends2, far_mid2c, far_mid2a],
        [
            (0, 32, 0, [(0, 0, 32, -1), (2, 0, 16, 31)]),
            (224, 32, 224, [(1, 64, 16, 220), (0, 32, 32, 226)]),
        ],
        sector,
        args,
        partial=1,
        kept=[(part3a, 32, 48), (part3b, 80, 64), (part3c, 144, 80)],
    )
    return merged[None]


def solution(mesh):
    in_specs = (
        P("sub", None, "sec", None),
        P("sub", None, None, None),
        P("sub", None, None, None, None),
        P("sub", None, None, None),
        P("sub", None, None),
    )
    out_specs = P("sub", None, "sec", None)
    return jax.shard_map(body, mesh=mesh, in_specs=in_specs, out_specs=out_specs, check_vma=False)
```
